512 devices in a mesh: sec: 4 (over y), tile: 128 (over x, z, core).
Axes of the slice: x: 4, y: 4, z: 16, core: 2. Of those that a mesh axis runs over, the one named last changes fastest.
Arguments:
- atm_flux: bfloat16 [20, 4194304], P(None, ('sec', 'tile')), may hold values from -6 to 6
- remap_rank: int32 [65536], P(('sec', 'tile')), may hold values from 0 to 127, as said below
- pair_src: int32 [98304], P('tile'), may hold values from 0 to 511, as said below
- pair_dst: int32 [98304], P('tile'), may hold values from 0 to 63, as said below
- pair_count: int32 [128], P('tile'), may hold values from 512 to 768, as said below
- pair_weight: bfloat16 [98304, 4096], P('tile'), may hold values from 0 to 1.5, as said below
- ocean_state: float32 [20, 524288], P('sec', 'tile'), may hold values from -6 to 6
- exchange_coef: float32 [20], P('sec'), may hold values from 0.2 to 1
- ocean_mask: int32 [524288], P('tile'), may hold values 0 or 1
Outputs:
- merged_flux: float32 [20, 524288], P('sec', 'tile')
The draws below stay inside these ranges and needn't reach their ends.
Inputs may be any that keep to these rules, and one draw needn't show every extreme that they name: `remap_rank`: among each device's 128 consecutive blocks, every tile index occurs exactly once. `pair_src`: the first 512 slots of each tile index name every assigned block once. `pair_dst`: the first 64 slots of each tile index name every destination block once. `pair_count`: some tile index has all 768 slots live. `pair_weight`: entries are nonnegative; each diagonal entry is at least 0.5.
All inputs are finite; a program needn't handle non-finite values. No bound on the sum of `ocean_mask` on one device may be relied on, other than what follows from the above.
Results may differ from the reference program's by a relative error of at most 0.0003.
Values may be sent and summed in bfloat16 or wider, within the bound.
A program may use at most 64 MiB of HBM per device.

```python
import math
import jax
import jax.numpy as jnp
from jax import lax

FLD = 20
BLK = 64
SRC_DEV = 128
DST_DEV = 64
PAIR_DEV = 768
A_BLOCKS = 65536
A_CELLS = 4194304
REMAP_BLK = 512
O_CELLS = 524288
N_SEC = 4
N_TILE = 128


def draw_remap_rank(key, part):
    key = jax.random.fold_in(key, 1)
    keys = jax.random.split(key, N_SEC * N_TILE)
    perms = jax.vmap(lambda single: jax.random.permutation(single, SRC_DEV))(keys)
    return (perms // (SRC_DEV // N_TILE)).reshape(-1).astype(jnp.int32)


def draw_pair_count(key, part):
    key = jax.random.fold_in(key, 2)
    keys = jax.random.split(key, 4)
    spread = PAIR_DEV - REMAP_BLK
    first = jax.random.randint(keys[0], (N_TILE,), 0, spread + 1)
    second = jax.random.randint(keys[1], (N_TILE,), 0, spread + 1)
    third = jax.random.randint(keys[2], (N_TILE,), 0, spread + 1)
    counts = REMAP_BLK + first * second // spread * third // spread
    busiest = jax.random.randint(keys[3], (), 0, N_TILE)
    return counts.at[busiest].set(PAIR_DEV).astype(jnp.int32)


def draw_pair_dst(key, part):
    key = jax.random.fold_in(key, 3)
    keys = jax.random.split(key, N_TILE)

    def one_tile(single):
        left, right = jax.random.split(single)
        covering = jax.random.permutation(left, DST_DEV)
        extra = jax.random.randint(right, (PAIR_DEV - DST_DEV,), 0, DST_DEV)
        return jnp.concatenate([covering, extra]).astype(jnp.int32)
    return jax.vmap(one_tile)(keys).reshape(-1)


def draw_pair_src(key, part):
    key = jax.random.fold_in(key, 4)
    keys = jax.random.split(key, N_TILE)

    def one_tile(single):
        left, right = jax.random.split(single)
        covering = jax.random.permutation(left, REMAP_BLK)
        extra = jax.random.randint(right, (PAIR_DEV - REMAP_BLK,), 0, REMAP_BLK)
        return jnp.concatenate([covering, extra]).astype(jnp.int32)
    return jax.vmap(one_tile)(keys).reshape(-1)


def draw_pair_weight(key, part):
    key = jax.random.fold_in(key, 5)
    left, right = jax.random.split(key)
    shape = (N_TILE * PAIR_DEV, BLK * BLK)
    flat = jnp.arange(BLK * BLK)
    diagonal = (flat // BLK == flat % BLK).astype(jnp.float32)[None, :]
    main = jnp.exp(jax.random.uniform(left, shape, jnp.float32, jnp.log(0.5), jnp.log(1.5)))
    side = jax.random.uniform(right, shape, jnp.float32, 0.0, 0.8 / BLK)
    return (diagonal * main + (1.0 - diagonal) * side).astype(jnp.bfloat16)


def touch_ends(entries, stream_key, least, top_value):
    shape = entries.shape
    index_at = [jax.random.randint(jax.random.fold_in(stream_key, axis), (), 0, shape[axis]) for axis in range(len(shape))]
    entries = entries.at[tuple(index_at)].set(least)
    longest = shape.index(max(shape))
    index_at[longest] = (index_at[longest] + 1) % shape[longest]
    return entries.at[tuple(index_at)].set(top_value)


def block_scale(stream_key, extent, cuts, smallest, largest):
    loudness = 1.0
    for axis_at, shards_of in cuts:
        steps = jax.random.uniform(jax.random.fold_in(jax.random.fold_in(stream_key, 6), axis_at), (shards_of,), jnp.float32, smallest / len(cuts), largest / len(cuts))
        loudness = loudness * jnp.repeat(jnp.exp(steps), extent[axis_at] // shards_of).reshape((-1,) + (1,) * (len(extent) - 1 - axis_at))
    return loudness


def normal_values(key, extent, scale, reach, cuts=(), kind=jnp.bfloat16):
    level = block_scale(key, extent, cuts, -0.22, 0.18) if cuts else 1.0
    drawn = jax.random.normal(key, extent, jnp.float32) * scale * level
    return jnp.minimum(jnp.maximum(drawn, -reach), reach).astype(kind)


def setup_inputs(seed: int = 0) -> dict:
    splits = jax.random.split(jax.random.key(seed), 10)
    atm_flux = normal_values(splits[0], (FLD, A_CELLS), 1.0, 6.0, ((1, 512),))
    remap_rank = draw_remap_rank(jax.random.fold_in(splits[9], 71), 0)
    pair_src = draw_pair_src(jax.random.fold_in(splits[9], 71), 0)
    pair_dst = draw_pair_dst(jax.random.fold_in(splits[9], 71), 0)
    pair_count = draw_pair_count(jax.random.fold_in(splits[9], 71), 0)
    pair_weight = draw_pair_weight(jax.random.fold_in(splits[9], 71), 0)
    ocean_state = normal_values(splits[6], (FLD, O_CELLS), 1.0, 6.0, ((0, 4), (1, 128)), jnp.float32)
    exchange_coef = jnp.clip(jnp.exp(math.log(1.0) - 1.609438 * jax.random.uniform(splits[7], (FLD,), jnp.float32) ** block_scale(splits[7], (FLD,), ((0, 4),), -0.2, 0.2)), 0.2, 1.0)
    ocean_mask = touch_ends((jax.random.randint(splits[8], (O_CELLS,), 0, 10) < 7).astype(jnp.int32), jax.random.fold_in(splits[8], 1), 0, 1)
    return {"atm_flux": atm_flux, "remap_rank": remap_rank, "pair_src": pair_src, "pair_dst": pair_dst, "pair_count": pair_count, "pair_weight": pair_weight, "ocean_state": ocean_state, "exchange_coef": exchange_coef, "ocean_mask": ocean_mask}


def remap_tile(sources, slot_src, slot_dst, weights, count):
    live_pairs = (jnp.arange(PAIR_DEV) < count).astype(jnp.float32)
    squares = weights.reshape(PAIR_DEV, BLK, BLK).astype(jnp.float32) * live_pairs[:, None, None]
    gathered = jnp.take(sources, slot_src, axis=1).astype(jnp.float32)
    contrib = jnp.einsum('fpi,pji->pfj', gathered, squares)
    summed = jax.ops.segment_sum(contrib, slot_dst, num_segments=DST_DEV)
    weight_rows = jax.ops.segment_sum(lax.optimization_barrier(jnp.sum(squares, axis=2)), slot_dst, num_segments=DST_DEV)
    remapped = summed / weight_rows[:, None, :]
    return jnp.transpose(remapped, (1, 0, 2)).reshape(FLD, DST_DEV * BLK)

def reference(atm_flux, remap_rank, pair_src, pair_dst, pair_count, pair_weight, ocean_state, exchange_coef, ocean_mask):
    blocks = atm_flux.reshape(FLD, A_BLOCKS, BLK)
    ranking = jnp.argsort(remap_rank, stable=True).astype(jnp.int32).reshape(N_TILE, REMAP_BLK)

    def per_tile(inputs):
        ranked, slot_src, slot_dst, weights, count = inputs
        sources = jnp.take(blocks, ranked, axis=1)
        return remap_tile(sources, slot_src, slot_dst, weights, count)
    tiles = lax.map(per_tile, (ranking, pair_src.reshape(N_TILE, PAIR_DEV), pair_dst.reshape(N_TILE, PAIR_DEV), pair_weight.reshape(N_TILE, PAIR_DEV, BLK * BLK), pair_count))
    remapped = jnp.transpose(tiles, (1, 0, 2)).reshape(FLD, O_CELLS)
    wind_speed = jnp.sqrt(remapped[0] * remapped[0] + remapped[1] * remapped[1] + 0.25)
    oceanic = ocean_mask.astype(jnp.float32)
    return remapped + oceanic[None, :] * exchange_coef[:, None] * wind_speed[None, :] * (ocean_state - remapped)
```

```python
import functools

import jax
import jax.numpy as jnp
from jax import lax
from jax.experimental import pallas as pl
from jax.experimental.pallas import tpu as pltpu
from jax.sharding import PartitionSpec as P

MESH = pl.DeviceIdType.MESH
F32, BF16, I32 = jnp.float32, jnp.bfloat16, jnp.int32
PAIRS, SOURCES, CELLS = 768, 512, 4096

OFFSETS = [8, 7, -7, 0, 6, -6, 5, -5, 4, -4, 3, -3, 2, -2, 1, -1]
PLACE = {dz: j for j, dz in enumerate(OFFSETS)}
CHUNKS = 4
SPAN = {0: (0, 1), 8: (15, 1)}
for _d in range(1, 8):
    SPAN[_d] = (2 * _d - 1, 2)


def iota(shape, dim):
    return lax.broadcasted_iota(I32, shape, dim)


def dot(a, b):
    return jnp.dot(a, b, preferred_element_type=F32)


def onehot(cond):
    return jnp.where(cond, 1.0, 0.0).astype(BF16)


def split(value):
    high = value.astype(BF16)
    return high, (value - high.astype(F32)).astype(BF16)


def kernel(
    x_ref, rank_ref, src_ref, dst_ref, count_ref, w_hbm, ocean_ref, coef_ref, mask_ref,
    out_ref,
    inv_v, inv_s, xpad, blocks, xsend, xrecv, units, zrecv, ysend, yrecv, wraw, wtile,
    field_rows, pack_rows, swap_rows, group_rows, dup_rows, keep, fill, select, expand,
    terms, sums, spread, final,
    inv_sem, w_sem, x_ss, x_rs, z_ss, z_rs, y_ss, y_rs,
):
    sec = lax.axis_index("sec")
    me = lax.axis_index("tile")
    x, z, c = me >> 5, (me >> 1) & 15, me & 1

    def tile_of(xx, zz, cc):
        return xx * 32 + zz * 2 + cc

    def peer(i):
        return tile_of(x ^ (i >> 1), z, c ^ (i & 1))

    def along(dz):
        return tile_of(x, (z + dz) & 15, c)

    barrier = pltpu.get_barrier_semaphore()
    for dz in OFFSETS:
        if dz:
            pl.semaphore_signal(
                barrier, inc=1, device_id={"tile": along(dz)}, device_id_type=MESH
            )
    for i in range(1, 8):
        pl.semaphore_signal(barrier, inc=1, device_id={"tile": peer(i)}, device_id_type=MESH)
    for i in range(1, 4):
        pl.semaphore_signal(barrier, inc=1, device_id={"sec": sec ^ i}, device_id_type=MESH)

    lane8 = iota((8, 128), 1)
    inv = jnp.zeros((8, 128), I32)
    for a in range(128):
        inv = jnp.where(lane8 == rank_ref[a], a, inv)
    inv_v[...] = inv
    inv_copy = pltpu.make_async_copy(inv_v, inv_s, inv_sem)
    inv_copy.start()

    w_copies = [
        pltpu.make_async_copy(
            w_hbm.at[pl.ds(128 * i, 128)], wraw.at[pl.ds(128 * i, 128)], w_sem.at[i]
        )
        for i in range(6)
    ]
    for copy in w_copies:
        copy.start()

    row, col = iota((32, 32), 0), iota((32, 32), 1)
    r, h = row & 15, row >> 4
    pair_field = 5 * (r >> 1) + 2 * (r & 1) + h
    last_field = 4 + 10 * (r - 8) + 5 * h
    wanted = jnp.where(r < 8, pair_field, last_field)
    field_rows[...] = onehot((col == wanted) & (r < 10))
    xpad[16:32, :] = jnp.zeros((16, 8192), BF16)
    xpad[0:16, :] = x_ref[0:16, :]
    xpad[16:20, :] = x_ref[16:20, :]

    low16 = iota((16, 128), 1) < 64

    def build(i, _):
        at = pl.multiple_of(i * 512, 512)
        packed = dot(field_rows[...], xpad[:, pl.ds(at, 512)])
        for q in range(4):
            a = packed[0:16, 128 * q : 128 * q + 128]
            b = packed[16:32, 128 * q : 128 * q + 128]
            blocks[i * 8 + 2 * q] = jnp.where(low16, a, pltpu.roll(b, 64, 1)).astype(BF16)
            blocks[i * 8 + 2 * q + 1] = jnp.where(low16, pltpu.roll(a, 64, 1), b).astype(BF16)
        return 0

    lax.fori_loop(0, 16, build, 0)

    row, col = iota((80, 128), 0), iota((80, 128), 1)
    pack_rows[...] = onehot(col == (row & 7) * 16 + (row >> 3))

    inv_copy.wait()
    x_copies = {}
    for chunk in range(CHUNKS):
        for i in range(8):
            for j in range(4 * chunk, 4 * chunk + 4):
                target = tile_of(x ^ (i >> 1), (z + OFFSETS[j]) & 15, c ^ (i & 1))
                block = blocks[inv_s[0, target]]
                if i == 0:
                    xrecv[0, j] = block
                else:
                    xsend[i, j] = block
        if chunk == 0:
            pl.semaphore_wait(barrier, 25)
        for i in (6, 7, 4, 5, 2, 3, 1):
            part = pl.ds(4 * chunk, 4)
            x_copies[i, chunk] = pltpu.make_async_remote_copy(
                xsend.at[i, part], xrecv.at[i, part], x_ss.at[i, chunk], x_rs.at[i, chunk],
                device_id={"tile": peer(i)}, device_id_type=MESH,
            )
            x_copies[i, chunk].start()

    row, col = iota((256, 256), 0), iota((256, 256), 1)
    swap_rows[...] = onehot(((row & 15) == (col >> 4)) & ((row >> 4) == (col & 15)))
    row, col = iota((128, 80), 0), iota((128, 80), 1)
    g, i8, r4 = sec ^ (row >> 5), (row >> 2) & 7, row & 3
    picked = jnp.where(r4 == 0, 0, jnp.where(r4 == 3, 8 + (g >> 1), 2 * g + r4 - 1))
    group_rows[...] = onehot(col == picked * 8 + i8)
    row, col = iota((128, 64), 0), iota((128, 64), 1)
    q = (row >> 2) & 3
    from_rolled = jnp.where((q == 1) | (q == 2), 32, 0)
    dup_rows[...] = onehot(col == from_rolled + (row >> 4) * 4 + (row & 3))
    row, col = iota((128, 256), 0), iota((128, 256), 1)
    inside = (((col & 127) < 64) == ((row & 15) < 8))
    unit_row = jnp.where((sec & 1) == 1, 3, 7)
    ones_here = inside & ((row & 7) == unit_row)
    keep[...] = jnp.where(inside & ((row & 7) != unit_row), 1.0, 0.0).astype(F32)
    fill[...] = jnp.where(ones_here, 1.0, 0.0).astype(F32)

    def compact(chunk):
        for i in range(1, 8):
            x_copies[i, chunk].wait_recv()
        for j in (4 * chunk, 4 * chunk + 2):
            both = jnp.concatenate(
                [xrecv[:, j].reshape(128, 128), xrecv[:, j + 1].reshape(128, 128)], axis=1
            )
            packed = dot(pack_rows[...], both).astype(BF16)
            units[j] = packed[:, :128]
            units[j + 1] = packed[:, 128:]

    z_copies = {}

    def send(j):
        dz = OFFSETS[j]
        if dz:
            z_copies[dz] = pltpu.make_async_remote_copy(
                units.at[j], zrecv.at[j], z_ss.at[j], z_rs.at[j],
                device_id={"tile": along(dz)}, device_id_type=MESH,
            )
            z_copies[dz].start()

    y_copies = {}

    def forward(d):
        at, n = SPAN[d]
        if d == 0:
            arrived = units[PLACE[0]]
        elif d == 8:
            z_copies[8].wait_recv()
            arrived = zrecv[PLACE[8]]
        else:
            z_copies[d].wait_recv()
            z_copies[-d].wait_recv()
            arrived = jnp.concatenate([zrecv[PLACE[d]], zrecv[PLACE[-d]]], axis=1)
        grouped = dot(group_rows[...], arrived).astype(BF16)
        for i in range(4):
            for u in range(n):
                piece = grouped[32 * i : 32 * i + 32, 128 * u : 128 * u + 128]
                if i == 0:
                    yrecv[0, at + u] = piece
                else:
                    ysend[i, at + u] = piece
        for i in (2, 1, 3):
            part = pl.ds(at, n)
            y_copies[i, d] = pltpu.make_async_remote_copy(
                ysend.at[i, part], yrecv.at[i, part], y_ss.at[i, d], y_rs.at[i, d],
                device_id={"sec": sec ^ i}, device_id_type=MESH,
            )
            y_copies[i, d].start()

    def place_sources(d, which):
        at, n = SPAN[d]
        for i in which:
            if i:
                y_copies[i, d].wait_recv()
            parts = []
            for u in range(n):
                plain = yrecv[i, at + u]
                rolled = pltpu.roll(plain.astype(F32), 64, 1).astype(BF16)
                parts.append(jnp.concatenate([plain, rolled], axis=0))
            both = parts[0] if n == 1 else jnp.concatenate(parts, axis=1)
            width = 128 * n
            made = dot(dup_rows[...], both) * keep[:, :width] + fill[:, :width]
            made = made.astype(BF16)
            for u in range(n):
                origin = (z + 16 - d) & 15 if u == 0 else (z + d) & 15
                for o in range(8):
                    slot = (sec ^ i) * 128 + tile_of(x ^ (o >> 1), origin, c ^ (o & 1))
                    sources_at(slot)[...] = made[16 * o : 16 * o + 16, 128 * u : 128 * u + 128]

    def sources_at(slot):
        return spread.at[slot]

    def weight_group(k, _):
        at = pl.multiple_of(k * 16, 16)
        pieces = [
            jnp.concatenate(
                [
                    wraw[pl.ds(at, 16), 128 * m : 128 * m + 128],
                    wraw[pl.ds(at, 16), 128 * (m + 16) : 128 * (m + 16) + 128],
                ],
                axis=1,
            )
            for m in range(16)
        ]
        made = dot(swap_rows[...], jnp.concatenate(pieces, axis=0)).astype(BF16)
        wtile[pl.ds(at, 16), 0:16, :] = made[:, :128].reshape(16, 16, 128)
        wtile[pl.ds(at, 16), 16:32, :] = made[:, 128:].reshape(16, 16, 128)
        return 0

    def weights(first, last):
        for i in range(6):
            if first <= 8 * i < last:
                w_copies[i].wait()
        lax.fori_loop(first, last, weight_group, 0)

    def selectors():
        row = iota((64, PAIRS), 0)
        dst = jnp.broadcast_to(dst_ref[...].reshape(1, PAIRS), (64, PAIRS))
        block = 2 * (row & 31) + (row >> 5)
        live = iota((64, PAIRS), 1) < count_ref[0]
        chosen = onehot((dst == block) & live)
        for g4 in range(4):
            row, col = iota((PAIRS, 384), 0), iota((PAIRS, 384), 1)
            n = col - jnp.where(col >= 192, 192, 0)
            thin = onehot(row == 4 * n + g4)
            select[64 * g4 : 64 * g4 + 64, :] = dot(chosen, thin).astype(BF16)
        row, col = iota((512, 128), 0), iota((512, 128), 1)
        j = 2 * (row & 31) + ((row >> 7) & 1)
        expand[...] = onehot(col == (row >> 8) * 64 + j)

    for chunk in range(CHUNKS):
        compact(chunk)
        for j in range(4 * chunk, 4 * chunk + 4):
            send(j)
    order = [0, 8, 7, 6, 5, 4, 3, 2, 1]
    done = 0
    selectors()
    for n, d in enumerate(order):
        forward(d)
        upto = min(48, done + 6)
        weights(done, upto)
        done = upto
        if n >= 2:
            place_sources(order[n - 2], (0, 1, 2, 3))
    for copy in x_copies.values():
        copy.wait_send()
    for copy in z_copies.values():
        copy.wait_send()
    for d in order[-2:]:
        place_sources(d, (0, 1, 2, 3))
    for copy in y_copies.values():
        copy.wait_send()

    lane = iota((16, 128), 1)

    def pair_tile(t, _):
        for s in range(4):
            k = (t * 4 + s) * 8
            left = jnp.concatenate([spread[src_ref[k + o]] for o in range(8)], axis=0)
            right = wtile[pl.ds(k, 8)].reshape(256, 128)
            made = lax.dot_general(
                left, right, (((1,), (1,)), ((), ())), preferred_element_type=F32
            )
            for q in range(2):
                part = [
                    made[64 * q + 16 * o : 64 * q + 16 * o + 16, 128 * q : 128 * q + 128]
                    for o in range(4)
                ]
                value = jnp.where(
                    lane < 64,
                    jnp.where(lane < 32, part[0], part[1]),
                    jnp.where(lane < 96, part[2], part[3]),
                )
                at = pl.multiple_of((2 * (t * 4 + s) + q) * 16, 16)
                terms[pl.ds(at, 16), :] = value
        return 0

    lax.fori_loop(0, 24, pair_tile, 0)

    lane = iota((64, 128), 1)
    odd = (sec & 1) == 1
    spot = {0: 5, 1: 0, 2: 2, 3: jnp.where(odd, 7, 4), 4: 6, 5: 1, 6: 3, 7: jnp.where(odd, 4, 7)}
    for r in range(0, 16, 2):
        sides = []
        for k in (r, r + 1):
            high, low = split(terms[pl.ds(k, 192, stride=16), :])
            sides.append(jnp.concatenate([high, low], axis=0))
        made = dot(select[...], jnp.concatenate(sides, axis=1))
        for o in range(2):
            part = [made[64 * g : 64 * g + 64, 128 * o : 128 * o + 128] for g in range(4)]
            value = jnp.where(
                lane < 64,
                jnp.where(lane < 32, part[0], part[1]),
                jnp.where(lane < 96, part[2], part[3]),
            )
            high, low = split(value)
            p, idx = (r + o) >> 3, (r + o) & 7
            at = spot[idx] * 32
            if not isinstance(at, int):
                at = pl.multiple_of(at, 32)
            for parity in range(2):
                lanes = pl.ds((parity * 2 + p) * 128, 128)
                sums[0, pl.ds(at, 32), lanes] = high[32 * parity : 32 * parity + 32]
                sums[1, pl.ds(at, 32), lanes] = low[32 * parity : 32 * parity + 32]
    final[...] = dot(sums[0], expand[...]) + dot(sums[1], expand[...])

    row8 = iota((8, 128), 0)
    coef = jnp.zeros((8, 128), F32)
    for f in range(5):
        coef = jnp.where(row8 == f, coef_ref[f], coef)
    coef = coef[0:5]
    wind = (row8 == 5) | (row8 == 6)
    oceanic = mask_ref[...].reshape(1, CELLS).astype(F32)
    for b in range(32):
        lanes = pl.ds(128 * b, 128)
        v = final[pl.ds(b, 8, stride=32), :]
        weight = jnp.broadcast_to(v[7:8], (8, 128))
        remapped = v / weight
        squares = jnp.where(wind, remapped * remapped, 0.0)
        speed = jnp.sqrt(jnp.sum(squares, axis=0, keepdims=True) + 0.25)
        own = remapped[0:5]
        factor = coef * (oceanic[:, 128 * b : 128 * b + 128] * speed)
        out_ref[:, lanes] = own + factor * (ocean_ref[:, lanes] - own)


def per_device(*args):
    vmem = pl.BlockSpec(memory_space=pltpu.VMEM)
    smem = pl.BlockSpec(memory_space=pltpu.SMEM)
    hbm = pl.BlockSpec(memory_space=pl.ANY)
    dma = pltpu.SemaphoreType.DMA
    return pl.pallas_call(
        kernel,
        out_shape=jax.ShapeDtypeStruct((5, CELLS), F32),
        in_specs=[vmem, smem, smem, vmem, smem, hbm, vmem, smem, vmem],
        out_specs=vmem,
        scratch_shapes=[
            pltpu.VMEM((8, 128), I32),
            pltpu.SMEM((8, 128), I32),
            pltpu.VMEM((32, 8192), BF16),
            pltpu.VMEM((128, 16, 128), BF16),
            pltpu.VMEM((8, 16, 16, 128), BF16),
            pltpu.VMEM((8, 16, 16, 128), BF16),
            pltpu.VMEM((16, 80, 128), BF16),
            pltpu.VMEM((16, 80, 128), BF16),
            pltpu.VMEM((4, 16, 32, 128), BF16),
            pltpu.VMEM((4, 16, 32, 128), BF16),
            pltpu.VMEM((PAIRS, 4096), BF16),
            pltpu.VMEM((PAIRS, 32, 128), BF16),
            pltpu.VMEM((32, 32), BF16),
            pltpu.VMEM((80, 128), BF16),
            pltpu.VMEM((256, 256), BF16),
            pltpu.VMEM((128, 80), BF16),
            pltpu.VMEM((128, 64), BF16),
            pltpu.VMEM((128, 256), F32),
            pltpu.VMEM((128, 256), F32),
            pltpu.VMEM((256, 384), BF16),
            pltpu.VMEM((512, 128), BF16),
            pltpu.VMEM((192 * 16, 128), F32),
            pltpu.VMEM((2, 256, 512), BF16),
            pltpu.VMEM((SOURCES, 16, 128), BF16),
            pltpu.VMEM((256, 128), F32),
            dma(()),
            dma((6,)),
            dma((8, CHUNKS)),
            dma((8, CHUNKS)),
            dma((16,)),
            dma((16,)),
            dma((4, 9)),
            dma((4, 9)),
        ],
        compiler_params=pltpu.CompilerParams(
            collective_id=0, has_side_effects=True, vmem_limit_bytes=48 * 2**20
        ),
    )(*args)


def solution(mesh):
    in_specs = (
        P(None, ("sec", "tile")),
        P(("sec", "tile")),
        P("tile"),
        P("tile"),
        P("tile"),
        P("tile", None),
        P("sec", "tile"),
        P("sec"),
        P("tile"),
    )
    return jax.shard_map(
        per_device, mesh=mesh, in_specs=in_specs, out_specs=P("sec", "tile"), check_vma=False
    )
```

```python
import functools

import jax
import jax.numpy as jnp
from jax import lax
from jax.experimental import pallas as pl
from jax.experimental.pallas import tpu as pltpu
from jax.sharding import PartitionSpec as P

MESH = pl.DeviceIdType.MESH
F32, BF16, I32 = jnp.float32, jnp.bfloat16, jnp.int32
PAIRS, SOURCES, CELLS = 768, 512, 4096

OFFSETS = [8, 1, -1, 0, 7, -7, 2, -2, 6, -6, 3, -3, 5, -5, 4, -4]
PLACE = {dz: j for j, dz in enumerate(OFFSETS)}
BOUNDS = [0, 4, 8, 12, 16]
CHUNKS = len(BOUNDS) - 1
FIRST, SECOND, EACH = 8, 28, 5
UNROLL = 16
SPAN = {0: (0, 1), 8: (15, 1)}
for _d in range(1, 8):
    SPAN[_d] = (2 * _d - 1, 2)


def iota(shape, dim):
    return lax.broadcasted_iota(I32, shape, dim)


def dot(a, b):
    return jnp.dot(a, b, preferred_element_type=F32)


def onehot(cond):
    return jnp.where(cond, 1.0, 0.0).astype(BF16)


def split(value):
    high = value.astype(BF16)
    return high, (value - high.astype(F32)).astype(BF16)


def kernel(
    x_hbm, rank_hbm, src_hbm, dst_hbm, count_hbm, w_hbm, ocean_hbm, coef_hbm, mask_hbm,
    out_ref,
    x_ref, rank_ref, src_ref, dst_ref, count_ref, ocean_ref, coef_ref, mask_ref, in_sem,
    inv_v, inv_s, xpad, blocks, xsend, xrecv, units, zrecv, ysend, yrecv, wraw, wtile,
    field_rows, pack_rows, swap_rows, group_rows, dup_rows, keep, fill, select, expand,
    terms, sums, spread, final,
    inv_sem, w_sem, x_ss, x_rs, z_ss, z_rs, y_ss, y_rs, known,
):
    sec = lax.axis_index("sec")
    me = lax.axis_index("tile")
    x, z, c = me >> 5, (me >> 1) & 15, me & 1

    def tile_of(xx, zz, cc):
        return xx * 32 + zz * 2 + cc

    def peer(i):
        return tile_of(x ^ (i >> 1), z, c ^ (i & 1))

    def along(dz):
        return tile_of(x, (z + dz) & 15, c)

    barrier = pltpu.get_barrier_semaphore()
    for dz in (2, -2, 1, -1):
        pl.semaphore_signal(barrier, inc=1, device_id={"tile": along(dz)}, device_id_type=MESH)
    for i in range(1, 8):
        pl.semaphore_signal(barrier, inc=1, device_id={"tile": peer(i)}, device_id_type=MESH)
    for i in range(1, 4):
        pl.semaphore_signal(barrier, inc=1, device_id={"sec": sec ^ i}, device_id_type=MESH)

    ins = [
        pltpu.make_async_copy(source, target, in_sem.at[i])
        for i, (source, target) in enumerate(
            [
                (rank_hbm, rank_ref), (x_hbm, x_ref), (src_hbm, src_ref), (dst_hbm, dst_ref),
                (count_hbm, count_ref), (coef_hbm, coef_ref), (mask_hbm, mask_ref),
                (ocean_hbm, ocean_ref),
            ]
        )
    ]
    for copy in ins:
        copy.start()

    ins[0].wait()
    lane8 = iota((8, 128), 1)
    inv = jnp.zeros((8, 128), I32)
    for a in range(128):
        inv = jnp.where(lane8 == rank_ref[a], a, inv)
    inv_v[...] = inv
    inv_copy = pltpu.make_async_copy(inv_v, inv_s, inv_sem)
    inv_copy.start()

    w_copies = [
        pltpu.make_async_copy(
            w_hbm.at[pl.ds(128 * i, 128)], wraw.at[pl.ds(128 * i, 128)], w_sem.at[i]
        )
        for i in range(6)
    ]
    for copy in w_copies:
        copy.start()

    row, col = iota((32, 32), 0), iota((32, 32), 1)
    r, h = row & 15, row >> 4
    pair_field = 5 * (r >> 1) + 2 * (r & 1) + h
    last_field = 4 + 10 * (r - 8) + 5 * h
    wanted = jnp.where(r < 8, pair_field, last_field)
    field_rows[...] = onehot((col == wanted) & (r < 10))
    xpad[16:32, :] = jnp.zeros((16, 8192), BF16)
    ins[1].wait()
    xpad[0:16, :] = x_ref[0:16, :]
    xpad[16:20, :] = x_ref[16:20, :]

    def tell(reach, which):
        for way, dz in enumerate((reach, -reach)):
            pl.semaphore_signal(
                known.at[which, way], inc=1, device_id={"tile": along(dz)}, device_id_type=MESH
            )

    def hear(which):
        for way in range(2):
            pl.semaphore_wait(known.at[which, way], 1)

    pl.semaphore_wait(barrier, 14)
    tell(2, 0)

    low16 = iota((16, 128), 1) < 64

    def build(i, _):
        at = pl.multiple_of(i * 512, 512)
        packed = dot(field_rows[...], xpad[:, pl.ds(at, 512)])
        for q in range(4):
            a = packed[0:16, 128 * q : 128 * q + 128]
            b = packed[16:32, 128 * q : 128 * q + 128]
            blocks[i * 8 + 2 * q] = jnp.where(low16, a, pltpu.roll(b, 64, 1)).astype(BF16)
            blocks[i * 8 + 2 * q + 1] = jnp.where(low16, pltpu.roll(a, 64, 1), b).astype(BF16)
        return 0

    lax.fori_loop(0, 16, build, 0)

    x_copies = {}

    def exchange(chunk):
        part = pl.ds(BOUNDS[chunk], BOUNDS[chunk + 1] - BOUNDS[chunk])
        for i in (6, 7, 4, 5, 2, 3, 1):
            x_copies[i, chunk] = pltpu.make_async_remote_copy(
                xsend.at[i, part], xrecv.at[i, part], x_ss.at[i, chunk], x_rs.at[i, chunk],
                device_id={"tile": peer(i)}, device_id_type=MESH,
            )
            x_copies[i, chunk].start()

    def compact(chunk):
        for i in range(1, 8):
            x_copies[i, chunk].wait_recv()
        for j in range(BOUNDS[chunk], BOUNDS[chunk + 1], 2):
            both = jnp.concatenate(
                [xrecv[:, j].reshape(128, 128), xrecv[:, j + 1].reshape(128, 128)], axis=1
            )
            packed = dot(pack_rows[...], both).astype(BF16)
            units[j] = packed[:, :128]
            units[j + 1] = packed[:, 128:]

    z_copies = {}

    def send(j):
        dz = OFFSETS[j]
        if dz:
            z_copies[dz] = pltpu.make_async_remote_copy(
                units.at[j], zrecv.at[j], z_ss.at[j], z_rs.at[j],
                device_id={"tile": along(dz)}, device_id_type=MESH,
            )
            z_copies[dz].start()

    y_copies = {}

    def forward(d):
        at, n = SPAN[d]
        if d == 0:
            arrived = units[PLACE[0]]
        elif d == 8:
            z_copies[8].wait_recv()
            arrived = zrecv[PLACE[8]]
        else:
            z_copies[d].wait_recv()
            z_copies[-d].wait_recv()
            arrived = jnp.concatenate([zrecv[PLACE[d]], zrecv[PLACE[-d]]], axis=1)
        grouped = dot(group_rows[...], arrived).astype(BF16)
        for i in range(4):
            for u in range(n):
                piece = grouped[32 * i : 32 * i + 32, 128 * u : 128 * u + 128]
                if i == 0:
                    yrecv[0, at + u] = piece
                else:
                    ysend[i, at + u] = piece
        for i in (2, 1, 3):
            part = pl.ds(at, n)
            y_copies[i, d] = pltpu.make_async_remote_copy(
                ysend.at[i, part], yrecv.at[i, part], y_ss.at[i, d], y_rs.at[i, d],
                device_id={"sec": sec ^ i}, device_id_type=MESH,
            )
            y_copies[i, d].start()

    def place_sources(d, which):
        at, n = SPAN[d]
        for i in which:
            if i:
                y_copies[i, d].wait_recv()
            parts = []
            for u in range(n):
                plain = yrecv[i, at + u]
                rolled = pltpu.roll(plain.astype(F32), 64, 1).astype(BF16)
                parts.append(jnp.concatenate([plain, rolled], axis=0))
            both = parts[0] if n == 1 else jnp.concatenate(parts, axis=1)
            width = 128 * n
            made = dot(dup_rows[...], both) * keep[:, :width] + fill[:, :width]
            made = made.astype(BF16)
            for u in range(n):
                origin = (z + 16 - d) & 15 if u == 0 else (z + d) & 15
                for o in range(8):
                    slot = (sec ^ i) * 128 + tile_of(x ^ (o >> 1), origin, c ^ (o & 1))
                    sources_at(slot)[...] = made[16 * o : 16 * o + 16, 128 * u : 128 * u + 128]

    def sources_at(slot):
        return spread.at[slot]

    def weight_group(k, _):
        at = pl.multiple_of(k * 16, 16)
        pieces = [
            jnp.concatenate(
                [
                    wraw[pl.ds(at, 16), 128 * m : 128 * m + 128],
                    wraw[pl.ds(at, 16), 128 * (m + 16) : 128 * (m + 16) + 128],
                ],
                axis=1,
            )
            for m in range(16)
        ]
        made = dot(swap_rows[...], jnp.concatenate(pieces, axis=0)).astype(BF16)
        wtile[pl.ds(at, 16), 0:16, :] = made[:, :128].reshape(16, 16, 128)
        wtile[pl.ds(at, 16), 16:32, :] = made[:, 128:].reshape(16, 16, 128)
        return 0

    def weights(first, last):
        if first == last:
            return
        for i in range(6):
            if first <= 8 * i < last:
                w_copies[i].wait()
        lax.fori_loop(first, last, weight_group, 0)

    def selectors():
        for copy in ins[2:]:
            copy.wait()
        row = iota((64, PAIRS), 0)
        dst = jnp.broadcast_to(dst_ref[...].reshape(1, PAIRS), (64, PAIRS))
        block = 2 * (row & 31) + (row >> 5)
        live = iota((64, PAIRS), 1) < count_ref[0]
        chosen = onehot((dst == block) & live)
        for g4 in range(4):
            row, col = iota((PAIRS, 384), 0), iota((PAIRS, 384), 1)
            n = col - jnp.where(col >= 192, 192, 0)
            thin = onehot(row == 4 * n + g4)
            select[64 * g4 : 64 * g4 + 64, :] = dot(chosen, thin).astype(BF16)
        row, col = iota((512, 128), 0), iota((512, 128), 1)
        j = 2 * (row & 31) + ((row >> 7) & 1)
        expand[...] = onehot(col == (row >> 8) * 64 + j)

    inv_copy.wait()
    for i in range(8):
        for j in range(16):
            target = tile_of(x ^ (i >> 1), (z + OFFSETS[j]) & 15, c ^ (i & 1))
            block = blocks[inv_s[0, target]]
            if i == 0:
                xrecv[0, j] = block
            else:
                xsend[i, j] = block
    hear(0)
    tell(4, 1)
    for chunk in range(CHUNKS):
        exchange(chunk)

    row, col = iota((80, 128), 0), iota((80, 128), 1)
    pack_rows[...] = onehot(col == (row & 7) * 16 + (row >> 3))


    row, col = iota((256, 256), 0), iota((256, 256), 1)
    swap_rows[...] = onehot(((row & 15) == (col >> 4)) & ((row >> 4) == (col & 15)))
    row, col = iota((128, 80), 0), iota((128, 80), 1)
    g, i8, r4 = sec ^ (row >> 5), (row >> 2) & 7, row & 3
    picked = jnp.where(r4 == 0, 0, jnp.where(r4 == 3, 8 + (g >> 1), 2 * g + r4 - 1))
    group_rows[...] = onehot(col == picked * 8 + i8)
    row, col = iota((128, 64), 0), iota((128, 64), 1)
    q = (row >> 2) & 3
    from_rolled = jnp.where((q == 1) | (q == 2), 32, 0)
    dup_rows[...] = onehot(col == from_rolled + (row >> 4) * 4 + (row & 3))
    row, col = iota((128, 256), 0), iota((128, 256), 1)
    inside = (((col & 127) < 64) == ((row & 15) < 8))
    unit_row = jnp.where((sec & 1) == 1, 3, 7)
    ones_here = inside & ((row & 7) == unit_row)
    keep[...] = jnp.where(inside & ((row & 7) != unit_row), 1.0, 0.0).astype(F32)
    fill[...] = jnp.where(ones_here, 1.0, 0.0).astype(F32)

    weights(0, FIRST)
    hear(1)
    for chunk in range(CHUNKS):
        compact(chunk)
        for j in range(BOUNDS[chunk], BOUNDS[chunk + 1]):
            send(j)
    order = [0, 1, 8, 2, 7, 3, 6, 4, 5]
    forward(0)
    weights(FIRST, SECOND)
    selectors()
    done = SECOND
    for n, d in enumerate(order):
        if n:
            forward(d)
            upto = min(48, done + EACH)
            weights(done, upto)
            done = upto
        if n >= 2:
            place_sources(order[n - 2], (0, 1, 2, 3))
    for copy in x_copies.values():
        copy.wait_send()
    for copy in z_copies.values():
        copy.wait_send()
    for d in order[-2:]:
        place_sources(d, (0, 1, 2, 3))
    for copy in y_copies.values():
        copy.wait_send()

    lane = iota((16, 128), 1)

    def pair_tile(t, _):
        for s in range(UNROLL):
            k = (t * UNROLL + s) * 8
            left = jnp.concatenate([spread[src_ref[k + o]] for o in range(8)], axis=0)
            right = wtile[pl.ds(k, 8)].reshape(256, 128)
            made = lax.dot_general(
                left, right, (((1,), (1,)), ((), ())), preferred_element_type=F32
            )
            for q in range(2):
                part = [
                    made[64 * q + 16 * o : 64 * q + 16 * o + 16, 128 * q : 128 * q + 128]
                    for o in range(4)
                ]
                value = jnp.where(
                    lane < 64,
                    jnp.where(lane < 32, part[0], part[1]),
                    jnp.where(lane < 96, part[2], part[3]),
                )
                at = pl.multiple_of((2 * (t * UNROLL + s) + q) * 16, 16)
                terms[pl.ds(at, 16), :] = value
        return 0

    lax.fori_loop(0, 96 // UNROLL, pair_tile, 0)

    lane = iota((64, 128), 1)
    odd = (sec & 1) == 1
    spot = {0: 5, 1: 0, 2: 2, 3: jnp.where(odd, 7, 4), 4: 6, 5: 1, 6: 3, 7: jnp.where(odd, 4, 7)}
    for r in range(0, 16, 2):
        sides = []
        for k in (r, r + 1):
            high, low = split(terms[pl.ds(k, 192, stride=16), :])
            sides.append(jnp.concatenate([high, low], axis=0))
        made = dot(select[...], jnp.concatenate(sides, axis=1))
        for o in range(2):
            part = [made[64 * g : 64 * g + 64, 128 * o : 128 * o + 128] for g in range(4)]
            value = jnp.where(
                lane < 64,
                jnp.where(lane < 32, part[0], part[1]),
                jnp.where(lane < 96, part[2], part[3]),
            )
            high, low = split(value)
            p, idx = (r + o) >> 3, (r + o) & 7
            at = spot[idx] * 32
            if not isinstance(at, int):
                at = pl.multiple_of(at, 32)
            for parity in range(2):
                lanes = pl.ds((parity * 2 + p) * 128, 128)
                sums[0, pl.ds(at, 32), lanes] = high[32 * parity : 32 * parity + 32]
                sums[1, pl.ds(at, 32), lanes] = low[32 * parity : 32 * parity + 32]
    final[...] = dot(sums[0], expand[...]) + dot(sums[1], expand[...])

    row8 = iota((8, 128), 0)
    coef = jnp.zeros((8, 128), F32)
    for f in range(5):
        coef = jnp.where(row8 == f, coef_ref[f], coef)
    coef = coef[0:5]
    wind = (row8 == 5) | (row8 == 6)
    oceanic = mask_ref[...].reshape(1, CELLS).astype(F32)
    for b in range(32):
        lanes = pl.ds(128 * b, 128)
        v = final[pl.ds(b, 8, stride=32), :]
        weight = jnp.broadcast_to(v[7:8], (8, 128))
        remapped = v / weight
        squares = jnp.where(wind, remapped * remapped, 0.0)
        speed = jnp.sqrt(jnp.sum(squares, axis=0, keepdims=True) + 0.25)
        own = remapped[0:5]
        factor = coef * (oceanic[:, 128 * b : 128 * b + 128] * speed)
        out_ref[:, lanes] = own + factor * (ocean_ref[:, lanes] - own)


def per_device(*args):
    vmem = pl.BlockSpec(memory_space=pltpu.VMEM)
    hbm = pl.BlockSpec(memory_space=pltpu.HBM)
    dma = pltpu.SemaphoreType.DMA
    return pl.pallas_call(
        kernel,
        out_shape=jax.ShapeDtypeStruct((5, CELLS), F32),
        in_specs=[hbm] * 9,
        out_specs=vmem,
        scratch_shapes=[
            pltpu.VMEM((20, 8192), BF16),
            pltpu.SMEM((128,), I32),
            pltpu.SMEM((PAIRS,), I32),
            pltpu.VMEM((PAIRS,), I32),
            pltpu.SMEM((1,), I32),
            pltpu.VMEM((5, CELLS), F32),
            pltpu.SMEM((5,), F32),
            pltpu.VMEM((CELLS,), I32),
            dma((8,)),
            pltpu.VMEM((8, 128), I32),
            pltpu.SMEM((8, 128), I32),
            pltpu.VMEM((32, 8192), BF16),
            pltpu.VMEM((128, 16, 128), BF16),
            pltpu.VMEM((8, 16, 16, 128), BF16),
            pltpu.VMEM((8, 16, 16, 128), BF16),
            pltpu.VMEM((16, 80, 128), BF16),
            pltpu.VMEM((16, 80, 128), BF16),
            pltpu.VMEM((4, 16, 32, 128), BF16),
            pltpu.VMEM((4, 16, 32, 128), BF16),
            pltpu.VMEM((PAIRS, 4096), BF16),
            pltpu.VMEM((PAIRS, 32, 128), BF16),
            pltpu.VMEM((32, 32), BF16),
            pltpu.VMEM((80, 128), BF16),
            pltpu.VMEM((256, 256), BF16),
            pltpu.VMEM((128, 80), BF16),
            pltpu.VMEM((128, 64), BF16),
            pltpu.VMEM((128, 256), F32),
            pltpu.VMEM((128, 256), F32),
            pltpu.VMEM((256, 384), BF16),
            pltpu.VMEM((512, 128), BF16),
            pltpu.VMEM((192 * 16, 128), F32),
            pltpu.VMEM((2, 256, 512), BF16),
            pltpu.VMEM((SOURCES, 16, 128), BF16),
            pltpu.VMEM((256, 128), F32),
            dma(()),
            dma((6,)),
            dma((8, CHUNKS)),
            dma((8, CHUNKS)),
            dma((16,)),
            dma((16,)),
            dma((4, 9)),
            dma((4, 9)),
            pltpu.SemaphoreType.REGULAR((2, 2)),
        ],
        compiler_params=pltpu.CompilerParams(
            collective_id=0, has_side_effects=True, vmem_limit_bytes=56 * 2**20
        ),
    )(*args)


def solution(mesh):
    in_specs = (
        P(None, ("sec", "tile")),
        P(("sec", "tile")),
        P("tile"),
        P("tile"),
        P("tile"),
        P("tile", None),
        P("sec", "tile"),
        P("sec"),
        P("tile"),
    )
    return jax.shard_map(
        per_device, mesh=mesh, in_specs=in_specs, out_specs=P("sec", "tile"), check_vma=False
    )
```

```python
import functools

import jax
import jax.numpy as jnp
from jax import lax
from jax.experimental import pallas as pl
from jax.experimental.pallas import tpu as pltpu
from jax.sharding import PartitionSpec as P

MESH = pl.DeviceIdType.MESH
F32, BF16, I32 = jnp.float32, jnp.bfloat16, jnp.int32
PAIRS, SOURCES, CELLS = 768, 512, 4096

OFFSETS = [8, 1, -1, 0, 7, -7, 2, -2, 6, -6, 3, -3, 5, -5, 4, -4]
PLACE = {dz: j for j, dz in enumerate(OFFSETS)}
BOUNDS = [0, 4, 10, 16]
CHUNKS = len(BOUNDS) - 1
FIRST, SECOND, EACH = 8, 28, 5
UNROLL = 32
SPAN = {0: (0, 1), 8: (15, 1)}
for _d in range(1, 8):
    SPAN[_d] = (2 * _d - 1, 2)


def iota(shape, dim):
    return lax.broadcasted_iota(I32, shape, dim)


def dot(a, b):
    return jnp.dot(a, b, preferred_element_type=F32)


def onehot(cond):
    return jnp.where(cond, 1.0, 0.0).astype(BF16)


def split(value):
    high = value.astype(BF16)
    return high, (value - high.astype(F32)).astype(BF16)


def kernel(
    x_hbm, rank_hbm, src_hbm, dst_hbm, count_hbm, w_hbm, ocean_hbm, coef_hbm, mask_hbm,
    out_ref,
    x_ref, rank_ref, src_ref, dst_ref, count_ref, ocean_ref, coef_ref, mask_ref, in_sem,
    inv_v, inv_s, xpad, blocks, xsend, xrecv, units, zrecv, ysend, yrecv, wraw, wtile,
    field_rows, pack_rows, swap_rows, group_rows, dup_rows, keep, fill, select, expand,
    terms, sums, spread, final,
    inv_sem, w_sem, x_ss, x_rs, z_ss, z_rs, y_ss, y_rs, known,
):
    sec = lax.axis_index("sec")
    me = lax.axis_index("tile")
    x, z, c = me >> 5, (me >> 1) & 15, me & 1

    def tile_of(xx, zz, cc):
        return xx * 32 + zz * 2 + cc

    def peer(i):
        return tile_of(x ^ (i >> 1), z, c ^ (i & 1))

    def along(dz):
        return tile_of(x, (z + dz) & 15, c)

    barrier = pltpu.get_barrier_semaphore()
    for dz in (2, -2, 1, -1):
        pl.semaphore_signal(barrier, inc=1, device_id={"tile": along(dz)}, device_id_type=MESH)
    for i in range(1, 8):
        pl.semaphore_signal(barrier, inc=1, device_id={"tile": peer(i)}, device_id_type=MESH)
    for i in range(1, 4):
        pl.semaphore_signal(barrier, inc=1, device_id={"sec": sec ^ i}, device_id_type=MESH)

    ins = [
        pltpu.make_async_copy(source, target, in_sem.at[i])
        for i, (source, target) in enumerate(
            [
                (rank_hbm, rank_ref), (x_hbm, x_ref), (src_hbm, src_ref), (dst_hbm, dst_ref),
                (count_hbm, count_ref), (coef_hbm, coef_ref), (mask_hbm, mask_ref),
                (ocean_hbm, ocean_ref),
            ]
        )
    ]
    for copy in ins:
        copy.start()

    ins[0].wait()
    lane8 = iota((8, 128), 1)
    inv = jnp.zeros((8, 128), I32)
    for a in range(128):
        inv = jnp.where(lane8 == rank_ref[a], a, inv)
    inv_v[...] = inv
    inv_copy = pltpu.make_async_copy(inv_v, inv_s, inv_sem)
    inv_copy.start()

    w_copies = [
        pltpu.make_async_copy(
            w_hbm.at[pl.ds(128 * i, 128)], wraw.at[pl.ds(128 * i, 128)], w_sem.at[i]
        )
        for i in range(6)
    ]
    for copy in w_copies:
        copy.start()

    row, col = iota((32, 32), 0), iota((32, 32), 1)
    r, h = row & 15, row >> 4
    pair_field = 5 * (r >> 1) + 2 * (r & 1) + h
    last_field = 4 + 10 * (r - 8) + 5 * h
    wanted = jnp.where(r < 8, pair_field, last_field)
    field_rows[...] = onehot((col == wanted) & (r < 10))
    xpad[16:32, :] = jnp.zeros((16, 8192), BF16)
    ins[1].wait()
    xpad[0:16, :] = x_ref[0:16, :]
    xpad[16:20, :] = x_ref[16:20, :]

    def tell(reach, which):
        for way, dz in enumerate((reach, -reach)):
            pl.semaphore_signal(
                known.at[which, way], inc=1, device_id={"tile": along(dz)}, device_id_type=MESH
            )

    def hear(which):
        for way in range(2):
            pl.semaphore_wait(known.at[which, way], 1)

    pl.semaphore_wait(barrier, 14)
    tell(2, 0)

    low16 = iota((16, 128), 1) < 64

    def build(i, _):
        at = pl.multiple_of(i * 512, 512)
        packed = dot(field_rows[...], xpad[:, pl.ds(at, 512)])
        for q in range(4):
            a = packed[0:16, 128 * q : 128 * q + 128]
            b = packed[16:32, 128 * q : 128 * q + 128]
            blocks[i * 8 + 2 * q] = jnp.where(low16, a, pltpu.roll(b, 64, 1)).astype(BF16)
            blocks[i * 8 + 2 * q + 1] = jnp.where(low16, pltpu.roll(a, 64, 1), b).astype(BF16)
        return 0

    lax.fori_loop(0, 16, build, 0)

    x_copies = {}

    def exchange(chunk):
        part = pl.ds(BOUNDS[chunk], BOUNDS[chunk + 1] - BOUNDS[chunk])
        for i in (6, 7, 4, 5, 2, 3, 1):
            x_copies[i, chunk] = pltpu.make_async_remote_copy(
                xsend.at[i, part], xrecv.at[i, part], x_ss.at[i, chunk], x_rs.at[i, chunk],
                device_id={"tile": peer(i)}, device_id_type=MESH,
            )
            x_copies[i, chunk].start()

    def compact(chunk):
        for i in range(1, 8):
            x_copies[i, chunk].wait_recv()
        for j in range(BOUNDS[chunk], BOUNDS[chunk + 1], 2):
            both = jnp.concatenate(
                [xrecv[:, j].reshape(128, 128), xrecv[:, j + 1].reshape(128, 128)], axis=1
            )
            packed = dot(pack_rows[...], both).astype(BF16)
            units[j] = packed[:, :128]
            units[j + 1] = packed[:, 128:]

    z_copies = {}

    def send(j):
        dz = OFFSETS[j]
        if dz:
            z_copies[dz] = pltpu.make_async_remote_copy(
                units.at[j], zrecv.at[j], z_ss.at[j], z_rs.at[j],
                device_id={"tile": along(dz)}, device_id_type=MESH,
            )
            z_copies[dz].start()

    y_copies = {}

    def forward(d):
        at, n = SPAN[d]
        if d == 0:
            arrived = units[PLACE[0]]
        elif d == 8:
            z_copies[8].wait_recv()
            arrived = zrecv[PLACE[8]]
        else:
            z_copies[d].wait_recv()
            z_copies[-d].wait_recv()
            arrived = jnp.concatenate([zrecv[PLACE[d]], zrecv[PLACE[-d]]], axis=1)
        grouped = dot(group_rows[...], arrived).astype(BF16)
        for i in range(4):
            for u in range(n):
                piece = grouped[32 * i : 32 * i + 32, 128 * u : 128 * u + 128]
                if i == 0:
                    yrecv[0, at + u] = piece
                else:
                    ysend[i, at + u] = piece
        for i in (2, 1, 3):
            part = pl.ds(at, n)
            y_copies[i, d] = pltpu.make_async_remote_copy(
                ysend.at[i, part], yrecv.at[i, part], y_ss.at[i, d], y_rs.at[i, d],
                device_id={"sec": sec ^ i}, device_id_type=MESH,
            )
            y_copies[i, d].start()

    def place_sources(d, which):
        at, n = SPAN[d]
        for i in which:
            if i:
                y_copies[i, d].wait_recv()
            parts = []
            for u in range(n):
                plain = yrecv[i, at + u]
                rolled = pltpu.roll(plain.astype(F32), 64, 1).astype(BF16)
                parts.append(jnp.concatenate([plain, rolled], axis=0))
            both = parts[0] if n == 1 else jnp.concatenate(parts, axis=1)
            width = 128 * n
            made = dot(dup_rows[...], both) * keep[:, :width] + fill[:, :width]
            made = made.astype(BF16)
            for u in range(n):
                origin = (z + 16 - d) & 15 if u == 0 else (z + d) & 15
                for o in range(8):
                    slot = (sec ^ i) * 128 + tile_of(x ^ (o >> 1), origin, c ^ (o & 1))
                    sources_at(slot)[...] = made[16 * o : 16 * o + 16, 128 * u : 128 * u + 128]

    def sources_at(slot):
        return spread.at[slot]

    def weight_group(k, _):
        at = pl.multiple_of(k * 16, 16)
        pieces = [
            jnp.concatenate(
                [
                    wraw[pl.ds(at, 16), 128 * m : 128 * m + 128],
                    wraw[pl.ds(at, 16), 128 * (m + 16) : 128 * (m + 16) + 128],
                ],
                axis=1,
            )
            for m in range(16)
        ]
        made = dot(swap_rows[...], jnp.concatenate(pieces, axis=0)).astype(BF16)
        wtile[pl.ds(at, 16), 0:16, :] = made[:, :128].reshape(16, 16, 128)
        wtile[pl.ds(at, 16), 16:32, :] = made[:, 128:].reshape(16, 16, 128)
        return 0

    def weights(first, last):
        if first == last:
            return
        for i in range(6):
            if first <= 8 * i < last:
                w_copies[i].wait()
        lax.fori_loop(first, last, weight_group, 0)

    def selectors():
        for copy in ins[2:]:
            copy.wait()
        row = iota((64, PAIRS), 0)
        dst = jnp.broadcast_to(dst_ref[...].reshape(1, PAIRS), (64, PAIRS))
        block = 2 * (row & 31) + (row >> 5)
        live = iota((64, PAIRS), 1) < count_ref[0]
        chosen = onehot((dst == block) & live)
        for g4 in range(4):
            row, col = iota((PAIRS, 384), 0), iota((PAIRS, 384), 1)
            n = col - jnp.where(col >= 192, 192, 0)
            thin = onehot(row == 4 * n + g4)
            select[64 * g4 : 64 * g4 + 64, :] = dot(chosen, thin).astype(BF16)
        row, col = iota((512, 128), 0), iota((512, 128), 1)
        j = 2 * (row & 31) + ((row >> 7) & 1)
        expand[...] = onehot(col == (row >> 8) * 64 + j)

    inv_copy.wait()
    for i in range(8):
        for j in range(16):
            target = tile_of(x ^ (i >> 1), (z + OFFSETS[j]) & 15, c ^ (i & 1))
            block = blocks[inv_s[0, target]]
            if i == 0:
                xrecv[0, j] = block
            else:
                xsend[i, j] = block
    hear(0)
    tell(4, 1)
    for chunk in range(CHUNKS):
        exchange(chunk)

    row, col = iota((80, 128), 0), iota((80, 128), 1)
    pack_rows[...] = onehot(col == (row & 7) * 16 + (row >> 3))


    row, col = iota((256, 256), 0), iota((256, 256), 1)
    swap_rows[...] = onehot(((row & 15) == (col >> 4)) & ((row >> 4) == (col & 15)))
    row, col = iota((128, 80), 0), iota((128, 80), 1)
    g, i8, r4 = sec ^ (row >> 5), (row >> 2) & 7, row & 3
    picked = jnp.where(r4 == 0, 0, jnp.where(r4 == 3, 8 + (g >> 1), 2 * g + r4 - 1))
    group_rows[...] = onehot(col == picked * 8 + i8)
    row, col = iota((128, 64), 0), iota((128, 64), 1)
    q = (row >> 2) & 3
    from_rolled = jnp.where((q == 1) | (q == 2), 32, 0)
    dup_rows[...] = onehot(col == from_rolled + (row >> 4) * 4 + (row & 3))
    row, col = iota((128, 256), 0), iota((128, 256), 1)
    inside = (((col & 127) < 64) == ((row & 15) < 8))
    unit_row = jnp.where((sec & 1) == 1, 3, 7)
    ones_here = inside & ((row & 7) == unit_row)
    keep[...] = jnp.where(inside & ((row & 7) != unit_row), 1.0, 0.0).astype(F32)
    fill[...] = jnp.where(ones_here, 1.0, 0.0).astype(F32)

    weights(0, FIRST)
    hear(1)
    for chunk in range(CHUNKS):
        compact(chunk)
        for j in range(BOUNDS[chunk], BOUNDS[chunk + 1]):
            send(j)
    order = [0, 1, 8, 2, 7, 3, 6, 4, 5]
    forward(0)
    weights(FIRST, SECOND)
    selectors()
    done = SECOND
    for n, d in enumerate(order):
        if n:
            forward(d)
            upto = min(48, done + EACH)
            weights(done, upto)
            done = upto
        if n >= 2:
            place_sources(order[n - 2], (0, 1, 2, 3))
    for copy in x_copies.values():
        copy.wait_send()
    for copy in z_copies.values():
        copy.wait_send()
    for d in order[-2:]:
        place_sources(d, (0, 1, 2, 3))
    for copy in y_copies.values():
        copy.wait_send()

    lane = iota((16, 128), 1)

    def pair_tile(t, _):
        for s in range(UNROLL):
            k = (t * UNROLL + s) * 8
            left = jnp.concatenate([spread[src_ref[k + o]] for o in range(8)], axis=0)
            right = wtile[pl.ds(k, 8)].reshape(256, 128)
            made = lax.dot_general(
                left, right, (((1,), (1,)), ((), ())), preferred_element_type=F32
            )
            for q in range(2):
                part = [
                    made[64 * q + 16 * o : 64 * q + 16 * o + 16, 128 * q : 128 * q + 128]
                    for o in range(4)
                ]
                value = jnp.where(
                    lane < 64,
                    jnp.where(lane < 32, part[0], part[1]),
                    jnp.where(lane < 96, part[2], part[3]),
                )
                at = pl.multiple_of((2 * (t * UNROLL + s) + q) * 16, 16)
                terms[pl.ds(at, 16), :] = value
        return 0

    lax.fori_loop(0, 96 // UNROLL, pair_tile, 0)

    lane = iota((64, 128), 1)
    odd = (sec & 1) == 1
    spot = {0: 5, 1: 0, 2: 2, 3: jnp.where(odd, 7, 4), 4: 6, 5: 1, 6: 3, 7: jnp.where(odd, 4, 7)}
    for r in range(0, 16, 2):
        sides = []
        for k in (r, r + 1):
            high, low = split(terms[pl.ds(k, 192, stride=16), :])
            sides.append(jnp.concatenate([high, low], axis=0))
        made = dot(select[...], jnp.concatenate(sides, axis=1))
        for o in range(2):
            part = [made[64 * g : 64 * g + 64, 128 * o : 128 * o + 128] for g in range(4)]
            value = jnp.where(
                lane < 64,
                jnp.where(lane < 32, part[0], part[1]),
                jnp.where(lane < 96, part[2], part[3]),
            )
            high, low = split(value)
            p, idx = (r + o) >> 3, (r + o) & 7
            at = spot[idx] * 32
            if not isinstance(at, int):
                at = pl.multiple_of(at, 32)
            for parity in range(2):
                lanes = pl.ds((parity * 2 + p) * 128, 128)
                sums[0, pl.ds(at, 32), lanes] = high[32 * parity : 32 * parity + 32]
                sums[1, pl.ds(at, 32), lanes] = low[32 * parity : 32 * parity + 32]
    final[...] = dot(sums[0], expand[...]) + dot(sums[1], expand[...])

    row8 = iota((8, 128), 0)
    coef = jnp.zeros((8, 128), F32)
    for f in range(5):
        coef = jnp.where(row8 == f, coef_ref[f], coef)
    coef = coef[0:5]
    wind = (row8 == 5) | (row8 == 6)
    oceanic = mask_ref[...].reshape(1, CELLS).astype(F32)
    for b in range(32):
        lanes = pl.ds(128 * b, 128)
        v = final[pl.ds(b, 8, stride=32), :]
        weight = jnp.broadcast_to(v[7:8], (8, 128))
        remapped = v / weight
        squares = jnp.where(wind, remapped * remapped, 0.0)
        speed = jnp.sqrt(jnp.sum(squares, axis=0, keepdims=True) + 0.25)
        own = remapped[0:5]
        factor = coef * (oceanic[:, 128 * b : 128 * b + 128] * speed)
        out_ref[:, lanes] = own + factor * (ocean_ref[:, lanes] - own)


def per_device(*args):
    vmem = pl.BlockSpec(memory_space=pltpu.VMEM)
    hbm = pl.BlockSpec(memory_space=pltpu.HBM)
    dma = pltpu.SemaphoreType.DMA
    return pl.pallas_call(
        kernel,
        out_shape=jax.ShapeDtypeStruct((5, CELLS), F32),
        in_specs=[hbm] * 9,
        out_specs=vmem,
        scratch_shapes=[
            pltpu.VMEM((20, 8192), BF16),
            pltpu.SMEM((128,), I32),
            pltpu.SMEM((PAIRS,), I32),
            pltpu.VMEM((PAIRS,), I32),
            pltpu.SMEM((1,), I32),
            pltpu.VMEM((5, CELLS), F32),
            pltpu.SMEM((5,), F32),
            pltpu.VMEM((CELLS,), I32),
            dma((8,)),
            pltpu.VMEM((8, 128), I32),
            pltpu.SMEM((8, 128), I32),
            pltpu.VMEM((32, 8192), BF16),
            pltpu.VMEM((128, 16, 128), BF16),
            pltpu.VMEM((8, 16, 16, 128), BF16),
            pltpu.VMEM((8, 16, 16, 128), BF16),
            pltpu.VMEM((16, 80, 128), BF16),
            pltpu.VMEM((16, 80, 128), BF16),
            pltpu.VMEM((4, 16, 32, 128), BF16),
            pltpu.VMEM((4, 16, 32, 128), BF16),
            pltpu.VMEM((PAIRS, 4096), BF16),
            pltpu.VMEM((PAIRS, 32, 128), BF16),
            pltpu.VMEM((32, 32), BF16),
            pltpu.VMEM((80, 128), BF16),
            pltpu.VMEM((256, 256), BF16),
            pltpu.VMEM((128, 80), BF16),
            pltpu.VMEM((128, 64), BF16),
            pltpu.VMEM((128, 256), F32),
            pltpu.VMEM((128, 256), F32),
            pltpu.VMEM((256, 384), BF16),
            pltpu.VMEM((512, 128), BF16),
            pltpu.VMEM((192 * 16, 128), F32),
            pltpu.VMEM((2, 256, 512), BF16),
            pltpu.VMEM((SOURCES, 16, 128), BF16),
            pltpu.VMEM((256, 128), F32),
            dma(()),
            dma((6,)),
            dma((8, CHUNKS)),
            dma((8, CHUNKS)),
            dma((16,)),
            dma((16,)),
            dma((4, 9)),
            dma((4, 9)),
            pltpu.SemaphoreType.REGULAR((2, 2)),
        ],
        compiler_params=pltpu.CompilerParams(
            collective_id=0, has_side_effects=True, vmem_limit_bytes=56 * 2**20
        ),
    )(*args)


def solution(mesh):
    in_specs = (
        P(None, ("sec", "tile")),
        P(("sec", "tile")),
        P("tile"),
        P("tile"),
        P("tile"),
        P("tile", None),
        P("sec", "tile"),
        P("sec"),
        P("tile"),
    )
    return jax.shard_map(
        per_device, mesh=mesh, in_specs=in_specs, out_specs=P("sec", "tile"), check_vma=False
    )
```

```python
import functools

import jax
import jax.numpy as jnp
from jax import lax
from jax.experimental import pallas as pl
from jax.experimental.pallas import tpu as pltpu
from jax.sharding import PartitionSpec as P

MESH = pl.DeviceIdType.MESH
F32, BF16, I32 = jnp.float32, jnp.bfloat16, jnp.int32
PAIRS, SOURCES, CELLS = 768, 512, 4096

OFFSETS = [8, 1, -1, 0, 7, -7, 2, -2, 6, -6, 3, -3, 5, -5, 4, -4]
PLACE = {dz: j for j, dz in enumerate(OFFSETS)}
BOUNDS = [0, 4, 10, 16]
CHUNKS = len(BOUNDS) - 1
FIRST, SECOND, EACH = 8, 28, 5
UNROLL = 32
SPAN = {0: (0, 1), 8: (15, 1)}
for _d in range(1, 8):
    SPAN[_d] = (2 * _d - 1, 2)


def iota(shape, dim):
    return lax.broadcasted_iota(I32, shape, dim)


def dot(a, b):
    return jnp.dot(a, b, preferred_element_type=F32)


def onehot(cond):
    return jnp.where(cond, 1.0, 0.0).astype(BF16)


def split(value):
    high = value.astype(BF16)
    return high, (value - high.astype(F32)).astype(BF16)


def kernel(
    x_hbm, rank_hbm, src_hbm, dst_hbm, count_hbm, w_hbm, ocean_hbm, coef_hbm, mask_hbm,
    out_ref,
    x_ref, rank_ref, src_ref, dst_ref, count_ref, ocean_ref, coef_ref, mask_ref, in_sem,
    inv_v, inv_s, xpad, blocks, xsend, xrecv, units, zrecv, ysend, yrecv, wraw, wtile,
    field_rows, pack_rows, swap_rows, group_rows, dup_rows, keep, fill, select, expand,
    terms, sums, spread, final,
    inv_sem, w_sem, x_ss, x_rs, z_ss, z_rs, y_ss, y_rs, known,
):
    sec = lax.axis_index("sec")
    me = lax.axis_index("tile")
    x, z, c = me >> 5, (me >> 1) & 15, me & 1

    def tile_of(xx, zz, cc):
        return xx * 32 + zz * 2 + cc

    def peer(i):
        return tile_of(x ^ (i >> 1), z, c ^ (i & 1))

    def along(dz):
        return tile_of(x, (z + dz) & 15, c)

    barrier = pltpu.get_barrier_semaphore()
    for dz in (2, -2, 1, -1):
        pl.semaphore_signal(barrier, inc=1, device_id={"tile": along(dz)}, device_id_type=MESH)
    for i in range(1, 8):
        pl.semaphore_signal(barrier, inc=1, device_id={"tile": peer(i)}, device_id_type=MESH)
    for i in range(1, 4):
        pl.semaphore_signal(barrier, inc=1, device_id={"sec": sec ^ i}, device_id_type=MESH)

    ins = [
        pltpu.make_async_copy(source, target, in_sem.at[i])
        for i, (source, target) in enumerate(
            [
                (rank_hbm, rank_ref), (x_hbm, x_ref), (src_hbm, src_ref), (dst_hbm, dst_ref),
                (count_hbm, count_ref), (coef_hbm, coef_ref), (mask_hbm, mask_ref),
                (ocean_hbm, ocean_ref),
            ]
        )
    ]
    for copy in ins:
        copy.start()

    ins[0].wait()
    lane8 = iota((8, 128), 1)
    inv = jnp.zeros((8, 128), I32)
    for a in range(128):
        inv = jnp.where(lane8 == rank_ref[a], a, inv)
    inv_v[...] = inv
    inv_copy = pltpu.make_async_copy(inv_v, inv_s, inv_sem)
    inv_copy.start()

    w_copies = [
        pltpu.make_async_copy(
            w_hbm.at[pl.ds(128 * i, 128)], wraw.at[pl.ds(128 * i, 128)], w_sem.at[i]
        )
        for i in range(6)
    ]
    for copy in w_copies:
        copy.start()

    row, col = iota((32, 32), 0), iota((32, 32), 1)
    r, h = row & 15, row >> 4
    pair_field = 5 * (r >> 1) + 2 * (r & 1) + h
    last_field = 4 + 10 * (r - 8) + 5 * h
    wanted = jnp.where(r < 8, pair_field, last_field)
    field_rows[...] = onehot((col == wanted) & (r < 10))
    xpad[16:32, :] = jnp.zeros((16, 8192), BF16)
    ins[1].wait()
    xpad[0:16, :] = x_ref[0:16, :]
    xpad[16:20, :] = x_ref[16:20, :]

    def tell(reach, which):
        for way, dz in enumerate((reach, -reach)):
            pl.semaphore_signal(
                known.at[which, way], inc=1, device_id={"tile": along(dz)}, device_id_type=MESH
            )

    def hear(which):
        for way in range(2):
            pl.semaphore_wait(known.at[which, way], 1)

    pl.semaphore_wait(barrier, 14)
    tell(2, 0)

    low16 = iota((16, 128), 1) < 64

    def build(i, _):
        at = pl.multiple_of(i * 512, 512)
        packed = dot(field_rows[...], xpad[:, pl.ds(at, 512)])
        for q in range(4):
            a = packed[0:16, 128 * q : 128 * q + 128]
            b = packed[16:32, 128 * q : 128 * q + 128]
            blocks[i * 8 + 2 * q] = jnp.where(low16, a, pltpu.roll(b, 64, 1)).astype(BF16)
            blocks[i * 8 + 2 * q + 1] = jnp.where(low16, pltpu.roll(a, 64, 1), b).astype(BF16)
        return 0

    lax.fori_loop(0, 16, build, 0)

    x_copies = {}

    def exchange(chunk):
        part = pl.ds(BOUNDS[chunk], BOUNDS[chunk + 1] - BOUNDS[chunk])
        for i in (6, 7, 4, 5, 2, 3, 1):
            x_copies[i, chunk] = pltpu.make_async_remote_copy(
                xsend.at[i, part], xrecv.at[i, part], x_ss.at[i, chunk], x_rs.at[i, chunk],
                device_id={"tile": peer(i)}, device_id_type=MESH,
            )
            x_copies[i, chunk].start()

    def compact(chunk):
        for i in range(1, 8):
            x_copies[i, chunk].wait_recv()
        for j in range(BOUNDS[chunk], BOUNDS[chunk + 1], 2):
            both = jnp.concatenate(
                [xrecv[:, j].reshape(128, 128), xrecv[:, j + 1].reshape(128, 128)], axis=1
            )
            packed = dot(pack_rows[...], both).astype(BF16)
            units[j] = packed[:, :128]
            units[j + 1] = packed[:, 128:]

    z_copies = {}

    def send(j):
        dz = OFFSETS[j]
        if dz:
            z_copies[dz] = pltpu.make_async_remote_copy(
                units.at[j], zrecv.at[j], z_ss.at[j], z_rs.at[j],
                device_id={"tile": along(dz)}, device_id_type=MESH,
            )
            z_copies[dz].start()

    y_copies = {}

    def forward(d):
        at, n = SPAN[d]
        if d == 0:
            arrived = units[PLACE[0]]
        elif d == 8:
            z_copies[8].wait_recv()
            arrived = zrecv[PLACE[8]]
        else:
            z_copies[d].wait_recv()
            z_copies[-d].wait_recv()
            arrived = jnp.concatenate([zrecv[PLACE[d]], zrecv[PLACE[-d]]], axis=1)
        grouped = dot(group_rows[...], arrived).astype(BF16)
        for i in range(4):
            for u in range(n):
                piece = grouped[32 * i : 32 * i + 32, 128 * u : 128 * u + 128]
                if i == 0:
                    yrecv[0, at + u] = piece
                else:
                    ysend[i, at + u] = piece
        for i in (2, 1, 3):
            part = pl.ds(at, n)
            y_copies[i, d] = pltpu.make_async_remote_copy(
                ysend.at[i, part], yrecv.at[i, part], y_ss.at[i, d], y_rs.at[i, d],
                device_id={"sec": sec ^ i}, device_id_type=MESH,
            )
            y_copies[i, d].start()

    def place_sources(d, which):
        at, n = SPAN[d]
        for i in which:
            if i:
                y_copies[i, d].wait_recv()
            parts = []
            for u in range(n):
                plain = yrecv[i, at + u]
                rolled = pltpu.roll(plain.astype(F32), 64, 1).astype(BF16)
                parts.append(jnp.concatenate([plain, rolled], axis=0))
            both = parts[0] if n == 1 else jnp.concatenate(parts, axis=1)
            width = 128 * n
            made = dot(dup_rows[...], both) * keep[:, :width] + fill[:, :width]
            made = made.astype(BF16)
            for u in range(n):
                origin = (z + 16 - d) & 15 if u == 0 else (z + d) & 15
                for o in range(8):
                    slot = (sec ^ i) * 128 + tile_of(x ^ (o >> 1), origin, c ^ (o & 1))
                    sources_at(slot)[...] = made[16 * o : 16 * o + 16, 128 * u : 128 * u + 128]

    def sources_at(slot):
        return spread.at[slot]

    def weight_group(k, _):
        at = pl.multiple_of(k * 16, 16)
        pieces = [
            jnp.concatenate(
                [
                    wraw[pl.ds(at, 16), 128 * m : 128 * m + 128],
                    wraw[pl.ds(at, 16), 128 * (m + 16) : 128 * (m + 16) + 128],
                ],
                axis=1,
            )
            for m in range(16)
        ]
        made = dot(swap_rows[...], jnp.concatenate(pieces, axis=0)).astype(BF16)
        wtile[pl.ds(at, 16), 0:16, :] = made[:, :128].reshape(16, 16, 128)
        wtile[pl.ds(at, 16), 16:32, :] = made[:, 128:].reshape(16, 16, 128)
        return 0

    def weights(first, last):
        if first == last:
            return
        for i in range(6):
            if first <= 8 * i < last:
                w_copies[i].wait()
        lax.fori_loop(first, last, weight_group, 0)

    def selectors():
        for copy in ins[2:]:
            copy.wait()
        row = iota((64, PAIRS), 0)
        dst = jnp.broadcast_to(dst_ref[...].reshape(1, PAIRS), (64, PAIRS))
        block = 2 * (row & 31) + (row >> 5)
        live = iota((64, PAIRS), 1) < count_ref[0]
        chosen = onehot((dst == block) & live)
        for g4 in range(4):
            row, col = iota((PAIRS, 384), 0), iota((PAIRS, 384), 1)
            n = col - jnp.where(col >= 192, 192, 0)
            thin = onehot(row == 4 * n + g4)
            select[64 * g4 : 64 * g4 + 64, :] = dot(chosen, thin).astype(BF16)
        row, col = iota((512, 128), 0), iota((512, 128), 1)
        j = 2 * (row & 31) + ((row >> 7) & 1)
        expand[...] = onehot(col == (row >> 8) * 64 + j)

    inv_copy.wait()
    for i in range(8):
        for j in range(16):
            target = tile_of(x ^ (i >> 1), (z + OFFSETS[j]) & 15, c ^ (i & 1))
            block = blocks[inv_s[0, target]]
            if i == 0:
                xrecv[0, j] = block
            else:
                xsend[i, j] = block
    hear(0)
    tell(4, 1)
    for chunk in range(CHUNKS):
        exchange(chunk)

    row, col = iota((80, 128), 0), iota((80, 128), 1)
    pack_rows[...] = onehot(col == (row & 7) * 16 + (row >> 3))


    row, col = iota((256, 256), 0), iota((256, 256), 1)
    swap_rows[...] = onehot(((row & 15) == (col >> 4)) & ((row >> 4) == (col & 15)))
    row, col = iota((128, 80), 0), iota((128, 80), 1)
    g, i8, r4 = sec ^ (row >> 5), (row >> 2) & 7, row & 3
    picked = jnp.where(r4 == 0, 0, jnp.where(r4 == 3, 8 + (g >> 1), 2 * g + r4 - 1))
    group_rows[...] = onehot(col == picked * 8 + i8)
    row, col = iota((128, 64), 0), iota((128, 64), 1)
    q = (row >> 2) & 3
    from_rolled = jnp.where((q == 1) | (q == 2), 32, 0)
    dup_rows[...] = onehot(col == from_rolled + (row >> 4) * 4 + (row & 3))
    row, col = iota((128, 256), 0), iota((128, 256), 1)
    inside = (((col & 127) < 64) == ((row & 15) < 8))
    unit_row = jnp.where((sec & 1) == 1, 3, 7)
    ones_here = inside & ((row & 7) == unit_row)
    keep[...] = jnp.where(inside & ((row & 7) != unit_row), 1.0, 0.0).astype(F32)
    fill[...] = jnp.where(ones_here, 1.0, 0.0).astype(F32)

    weights(0, FIRST)
    hear(1)
    for chunk in range(CHUNKS):
        compact(chunk)
        for j in range(BOUNDS[chunk], BOUNDS[chunk + 1]):
            send(j)
    order = [0, 1, 8, 2, 7, 3, 6, 4, 5]
    forward(0)
    weights(FIRST, SECOND)
    selectors()
    done = SECOND
    for n, d in enumerate(order):
        if n:
            forward(d)
            upto = min(48, done + EACH)
            weights(done, upto)
            done = upto
        if n >= 2:
            place_sources(order[n - 2], (0, 1, 2, 3))
    for copy in x_copies.values():
        copy.wait_send()
    for copy in z_copies.values():
        copy.wait_send()
    for d in order[-2:]:
        place_sources(d, (0,))
    for copy in y_copies.values():
        copy.wait_send()
    for d in order[-2:]:
        place_sources(d, (1, 3, 2))

    lane = iota((16, 128), 1)

    def pair_tile(t, _):
        for s in range(UNROLL):
            k = (t * UNROLL + s) * 8
            left = jnp.concatenate([spread[src_ref[k + o]] for o in range(8)], axis=0)
            right = wtile[pl.ds(k, 8)].reshape(256, 128)
            made = lax.dot_general(
                left, right, (((1,), (1,)), ((), ())), preferred_element_type=F32
            )
            for q in range(2):
                part = [
                    made[64 * q + 16 * o : 64 * q + 16 * o + 16, 128 * q : 128 * q + 128]
                    for o in range(4)
                ]
                value = jnp.where(
                    lane < 64,
                    jnp.where(lane < 32, part[0], part[1]),
                    jnp.where(lane < 96, part[2], part[3]),
                )
                at = pl.multiple_of((2 * (t * UNROLL + s) + q) * 16, 16)
                terms[pl.ds(at, 16), :] = value
        return 0

    lax.fori_loop(0, 96 // UNROLL, pair_tile, 0)

    lane = iota((64, 128), 1)
    odd = (sec & 1) == 1
    spot = {0: 5, 1: 0, 2: 2, 3: jnp.where(odd, 7, 4), 4: 6, 5: 1, 6: 3, 7: jnp.where(odd, 4, 7)}
    for r in range(0, 16, 2):
        sides = []
        for k in (r, r + 1):
            high, low = split(terms[pl.ds(k, 192, stride=16), :])
            sides.append(jnp.concatenate([high, low], axis=0))
        made = dot(select[...], jnp.concatenate(sides, axis=1))
        for o in range(2):
            part = [made[64 * g : 64 * g + 64, 128 * o : 128 * o + 128] for g in range(4)]
            value = jnp.where(
                lane < 64,
                jnp.where(lane < 32, part[0], part[1]),
                jnp.where(lane < 96, part[2], part[3]),
            )
            high, low = split(value)
            p, idx = (r + o) >> 3, (r + o) & 7
            at = spot[idx] * 32
            if not isinstance(at, int):
                at = pl.multiple_of(at, 32)
            for parity in range(2):
                lanes = pl.ds((parity * 2 + p) * 128, 128)
                sums[0, pl.ds(at, 32), lanes] = high[32 * parity : 32 * parity + 32]
                sums[1, pl.ds(at, 32), lanes] = low[32 * parity : 32 * parity + 32]
    final[...] = dot(sums[0], expand[...]) + dot(sums[1], expand[...])

    row8 = iota((8, 128), 0)
    coef = jnp.zeros((8, 128), F32)
    for f in range(5):
        coef = jnp.where(row8 == f, coef_ref[f], coef)
    coef = coef[0:5]
    wind = (row8 == 5) | (row8 == 6)
    oceanic = mask_ref[...].reshape(1, CELLS).astype(F32)
    for b in range(32):
        lanes = pl.ds(128 * b, 128)
        v = final[pl.ds(b, 8, stride=32), :]
        weight = jnp.broadcast_to(v[7:8], (8, 128))
        remapped = v / weight
        squares = jnp.where(wind, remapped * remapped, 0.0)
        speed = jnp.sqrt(jnp.sum(squares, axis=0, keepdims=True) + 0.25)
        own = remapped[0:5]
        factor = coef * (oceanic[:, 128 * b : 128 * b + 128] * speed)
        out_ref[:, lanes] = own + factor * (ocean_ref[:, lanes] - own)


def per_device(*args):
    vmem = pl.BlockSpec(memory_space=pltpu.VMEM)
    hbm = pl.BlockSpec(memory_space=pltpu.HBM)
    dma = pltpu.SemaphoreType.DMA
    return pl.pallas_call(
        kernel,
        out_shape=jax.ShapeDtypeStruct((5, CELLS), F32),
        in_specs=[hbm] * 9,
        out_specs=vmem,
        scratch_shapes=[
            pltpu.VMEM((20, 8192), BF16),
            pltpu.SMEM((128,), I32),
            pltpu.SMEM((PAIRS,), I32),
            pltpu.VMEM((PAIRS,), I32),
            pltpu.SMEM((1,), I32),
            pltpu.VMEM((5, CELLS), F32),
            pltpu.SMEM((5,), F32),
            pltpu.VMEM((CELLS,), I32),
            dma((8,)),
            pltpu.VMEM((8, 128), I32),
            pltpu.SMEM((8, 128), I32),
            pltpu.VMEM((32, 8192), BF16),
            pltpu.VMEM((128, 16, 128), BF16),
            pltpu.VMEM((8, 16, 16, 128), BF16),
            pltpu.VMEM((8, 16, 16, 128), BF16),
            pltpu.VMEM((16, 80, 128), BF16),
            pltpu.VMEM((16, 80, 128), BF16),
            pltpu.VMEM((4, 16, 32, 128), BF16),
            pltpu.VMEM((4, 16, 32, 128), BF16),
            pltpu.VMEM((PAIRS, 4096), BF16),
            pltpu.VMEM((PAIRS, 32, 128), BF16),
            pltpu.VMEM((32, 32), BF16),
            pltpu.VMEM((80, 128), BF16),
            pltpu.VMEM((256, 256), BF16),
            pltpu.VMEM((128, 80), BF16),
            pltpu.VMEM((128, 64), BF16),
            pltpu.VMEM((128, 256), F32),
            pltpu.VMEM((128, 256), F32),
            pltpu.VMEM((256, 384), BF16),
            pltpu.VMEM((512, 128), BF16),
            pltpu.VMEM((192 * 16, 128), F32),
            pltpu.VMEM((2, 256, 512), BF16),
            pltpu.VMEM((SOURCES, 16, 128), BF16),
            pltpu.VMEM((256, 128), F32),
            dma(()),
            dma((6,)),
            dma((8, CHUNKS)),
            dma((8, CHUNKS)),
            dma((16,)),
            dma((16,)),
            dma((4, 9)),
            dma((4, 9)),
            pltpu.SemaphoreType.REGULAR((2, 2)),
        ],
        compiler_params=pltpu.CompilerParams(
            collective_id=0, has_side_effects=True, vmem_limit_bytes=56 * 2**20
        ),
    )(*args)


def solution(mesh):
    in_specs = (
        P(None, ("sec", "tile")),
        P(("sec", "tile")),
        P("tile"),
        P("tile"),
        P("tile"),
        P("tile", None),
        P("sec", "tile"),
        P("sec"),
        P("tile"),
    )
    return jax.shard_map(
        per_device, mesh=mesh, in_specs=in_specs, out_specs=P("sec", "tile"), check_vma=False
    )
```
